128 devices in a mesh: group: 8 (over x_hi, y), resp: 16 (over z, x_lo, core).
Axes of the slice: x: 4 (x_hi: 2, x_lo: 2; x = x_hi * 2 + x_lo), y: 4, z: 4, core: 2. Of those that a mesh axis runs over, the one named last changes fastest.
Arguments:
- query_raw: bfloat16 [8, 16, 256, 4096], P('group', 'resp')
- key_raw: bfloat16 [8, 16, 256, 512], P('group', 'resp')
- response_values: bfloat16 [8, 16, 256, 512], P('group', 'resp'), may hold values from -6 to 6
- prompt_keys: bfloat16 [8, 16, 1792, 512], P('group', 'resp'), may hold values from -6 to 6
- prompt_values: bfloat16 [8, 16, 1792, 512], P('group', 'resp'), may hold values from -6 to 6
- grad_output: bfloat16 [8, 16, 256, 4096], P('group', 'resp'), may hold values from -6 to 6
- query_gain: float32 [128], replicated, may hold values from 0.6 to 6
- key_gain: float32 [128], replicated, may hold values from 0.6 to 6
- lengths: int32 [8, 16], P('group', 'resp'), may hold values from 1 to 256, as said below
- owner: int32 [8], P('group'), may hold values from 0 to 15
Outputs:
- query_grad: bfloat16 [8, 16, 256, 4096], P('group', 'resp')
- key_grad: bfloat16 [8, 16, 256, 512], P('group', 'resp')
- value_grad: bfloat16 [8, 16, 256, 512], P('group', 'resp')
- prompt_key_grad: bfloat16 [8, 16, 1792, 512], P('group', 'resp')
- prompt_value_grad: bfloat16 [8, 16, 1792, 512], P('group', 'resp')
- gain_grads: float32 [2, 128], replicated
The draws below stay inside these ranges and needn't reach their ends.
Inputs may be any that keep to these rules, and one draw needn't show every extreme that they name: `lengths`: some response of every group has all 256 tokens live.
All inputs are finite; a program needn't handle non-finite values.
Results may differ from the reference program's by a relative error of at most 0.018.
The reference program's roundings to bfloat16 on the way count: a program that leaves them out, or rounds other values in their place, can miss the bound.
Values may be sent and summed in bfloat16 or wider, within the bound.
A program may use at most 128 MiB of HBM per device.

```python
import jax
import jax.numpy as jnp
from jax import lax

DH = 128
QH = 32
KVH = 4
P_SIZE = 1792
L = 256
GROUPS = 8
RESPS = 16


def shared_keys(key):
    return jax.random.normal(key, (GROUPS, RESPS, L, KVH * DH), jnp.float32)


def draw_key_raw(key, part):
    values = shared_keys(key)
    return values.astype(jnp.bfloat16)


def draw_query_raw(key, part):
    key = jax.random.fold_in(key, 11)
    return jax.random.normal(key, (GROUPS, RESPS, L, QH * DH), jnp.float32).astype(jnp.bfloat16)


def draw_query_gain(key, part):
    key = jax.random.fold_in(key, 21)
    return jax.random.uniform(key, (DH,), jnp.float32, 0.6, 1.8)


def draw_key_gain(key, part):
    key = jax.random.fold_in(key, 31)
    return jax.random.uniform(key, (DH,), jnp.float32, 0.6, 1.8)


def draw_lengths(key, part):
    key = jax.random.fold_in(key, 41)
    cap_key, length_key, slot_key = jax.random.split(key, 3)
    caps = jax.random.randint(cap_key, (GROUPS, 1), L // 2, L + 1, dtype=jnp.int32)
    drawn = jax.random.randint(length_key, (GROUPS, RESPS), 1, caps + 1, dtype=jnp.int32)
    full_slot = jax.random.randint(slot_key, (GROUPS, 1), 0, RESPS, dtype=jnp.int32)
    slots = jnp.arange(RESPS, dtype=jnp.int32)[None, :]
    return jnp.where(slots == full_slot, jnp.int32(L), drawn).astype(jnp.int32)


def touch_ends(result, key, smallest, largest):
    longest = result.shape.index(max(result.shape))
    spots = []
    for shift in (0, 1):
        where = [jax.random.randint(jax.random.fold_in(key, axis), (), 0, length) for axis, length in enumerate(result.shape)]
        where[longest] = (where[longest] + shift) % result.shape[longest]
        spots.append(tuple(where))
    return result.at[spots[0]].set(smallest).at[spots[1]].set(largest)


def level_of(rng, shape, cuts, low, high):
    loudness, own = 1.0, jax.random.fold_in(rng, 6)
    for axis_at, shards_of in cuts:
        steps = jnp.exp(jax.random.uniform(jax.random.fold_in(own, axis_at), (shards_of,), jnp.float32, low / len(cuts), high / len(cuts)))
        loudness = loudness * jnp.repeat(steps, shape[axis_at] // shards_of).reshape([-1 if axis == axis_at else 1 for axis in range(len(shape))])
    return loudness


def gaussian(stream_key, dims, width, bound, cuts=(), kind=jnp.bfloat16):
    result = jax.random.normal(stream_key, dims, jnp.float32) * width
    if len(cuts) > 0:
        result = level_of(stream_key, dims, cuts, -0.22, 0.18) * result
    return jnp.clip(result, min=-bound, max=bound).astype(kind)


def setup_inputs(seed: int = 0) -> dict:
    streams_of = jax.random.split(jax.random.key(seed), 11)
    query_raw = draw_query_raw(jax.random.fold_in(streams_of[10], 71), 0)
    key_raw = draw_key_raw(jax.random.fold_in(streams_of[10], 71), 0)
    response_values = gaussian(streams_of[2], (GROUPS, RESPS, L, KVH * DH), 1.0, 6.0, ((0, 8), (1, 16)))
    prompt_keys = gaussian(streams_of[3], (GROUPS, RESPS, P_SIZE, KVH * DH), 1.0, 6.0, ((0, 8), (1, 16)))
    prompt_values = gaussian(streams_of[4], (GROUPS, RESPS, P_SIZE, KVH * DH), 1.0, 6.0, ((0, 8), (1, 16)))
    grad_output = gaussian(streams_of[5], (GROUPS, RESPS, L, QH * DH), 1.0, 6.0, ((0, 8), (1, 16)))
    query_gain = draw_query_gain(jax.random.fold_in(streams_of[10], 71), 0)
    key_gain = draw_key_gain(jax.random.fold_in(streams_of[10], 71), 0)
    lengths = draw_lengths(jax.random.fold_in(streams_of[10], 71), 0)
    owner = touch_ends(jax.random.randint(streams_of[9], (GROUPS,), 0, RESPS), jax.random.fold_in(streams_of[9], 1), 0, RESPS - 1).astype(jnp.int32)
    return {"query_raw": query_raw, "key_raw": key_raw, "response_values": response_values, "prompt_keys": prompt_keys, "prompt_values": prompt_values, "grad_output": grad_output, "query_gain": query_gain, "key_gain": key_gain, "lengths": lengths, "owner": owner}


epsilon = 1e-06

def normalize(raw, gain):
    values = raw.astype(jnp.float32).reshape(raw.shape[0], -1, DH)
    inverse = lax.rsqrt(lax.optimization_barrier(jnp.mean(values * values, axis=-1, keepdims=True)) + epsilon)
    unit = values * inverse
    return (unit, inverse, (unit * gain).astype(jnp.bfloat16))

def norm_back(grad_normed, unit, inverse, gain):
    grad_unit = grad_normed * gain
    grad_raw = (grad_unit - unit * lax.optimization_barrier(jnp.mean(grad_unit * unit, axis=-1, keepdims=True))) * inverse
    return (grad_raw.reshape(grad_raw.shape[0], -1), lax.optimization_barrier(jnp.sum(grad_normed * unit, axis=(0, 1))))

def attend_back(queries, key_rows, value_rows, grad_out):
    count = queries.shape[0]
    total = key_rows.shape[0]
    allowed = jnp.arange(total, dtype=jnp.int32)[None, :] - (total - count) <= jnp.arange(count, dtype=jnp.int32)[:, None]
    factor = DH ** (-0.5)

    def one_head(carry, head):
        grad_keys, grad_values = carry
        shared = head // (QH // KVH)
        query = lax.dynamic_index_in_dim(queries, head, 1, keepdims=False)
        out_head = lax.dynamic_index_in_dim(grad_out, head, 1, keepdims=False)
        key_block = lax.dynamic_index_in_dim(key_rows, shared, 1, keepdims=False)
        value_block = lax.dynamic_index_in_dim(value_rows, shared, 1, keepdims=False)
        scores = jnp.dot(query, key_block.T, preferred_element_type=jnp.float32) * factor
        scores = jnp.where(allowed, scores, -jnp.inf)
        peak = lax.optimization_barrier(jnp.max(scores, axis=-1, keepdims=True))
        exponent = jnp.exp(scores - peak)
        probs = exponent / lax.optimization_barrier(jnp.sum(exponent, axis=-1, keepdims=True))
        probs_low = probs.astype(jnp.bfloat16)
        outputs = jnp.dot(probs_low, value_block, preferred_element_type=jnp.float32)
        row_dots = lax.optimization_barrier(jnp.sum(out_head.astype(jnp.float32) * outputs, axis=-1))
        grad_probs = jnp.dot(out_head, value_block.T, preferred_element_type=jnp.float32)
        grad_scores = (probs * (grad_probs - row_dots[:, None]) * factor).astype(jnp.bfloat16)
        grad_query = jnp.dot(grad_scores, key_block, preferred_element_type=jnp.float32)
        key_add = jnp.dot(grad_scores.T, query, preferred_element_type=jnp.float32)
        value_add = jnp.dot(probs_low.T, out_head, preferred_element_type=jnp.float32)
        grad_keys = grad_keys.at[shared].add(key_add)
        grad_values = grad_values.at[shared].add(value_add)
        return ((grad_keys, grad_values), grad_query)
    empty = jnp.zeros((KVH, total, DH), jnp.float32)
    (grad_keys, grad_values), grad_queries = lax.scan(one_head, (empty, empty), jnp.arange(QH, dtype=jnp.int32))
    return (jnp.moveaxis(grad_queries, 0, 1), jnp.moveaxis(grad_keys, 0, 1), jnp.moveaxis(grad_values, 0, 1))

def reference(query_raw, key_raw, response_values, prompt_keys, prompt_values, grad_output, query_gain, key_gain, lengths, owner):
    positions = jnp.arange(L, dtype=jnp.int32)

    def per_group(items):
        query_group, key_group, value_group, pkey_group, pvalue_group, out_group, length_group, chosen = items
        prompt_key = lax.dynamic_index_in_dim(pkey_group, chosen, 0, keepdims=False)
        prompt_value = lax.dynamic_index_in_dim(pvalue_group, chosen, 0, keepdims=False)
        p_unit, p_inverse, p_normed = normalize(prompt_key, key_gain)
        scaling = RESPS * L / jnp.sum(length_group.astype(jnp.float32))

        def per_response(carry, parts):
            key_sum, value_sum, query_part, key_part = carry
            query_one, key_one, value_one, out_one, length_one = parts
            query_unit, query_inverse, query_normed = normalize(query_one, query_gain)
            key_unit, key_inverse, key_normed = normalize(key_one, key_gain)
            live = (positions < length_one)[:, None]
            grad_out = (out_one.astype(jnp.float32) * live * scaling).astype(jnp.bfloat16).reshape(L, QH, DH)
            key_rows = jnp.concatenate([p_normed, key_normed], axis=0)
            value_rows = jnp.concatenate([prompt_value, value_one], axis=0).reshape(P_SIZE + L, KVH, DH)
            grad_query, grad_keys, grad_values = attend_back(query_normed, key_rows, value_rows, grad_out)
            query_grad, query_add = norm_back(grad_query, query_unit, query_inverse, query_gain)
            key_grad, key_add = norm_back(grad_keys[P_SIZE:], key_unit, key_inverse, key_gain)
            grad_values = grad_values.reshape(P_SIZE + L, KVH * DH)
            carry = (key_sum + grad_keys[:P_SIZE], value_sum + grad_values[:P_SIZE], query_part + query_add, key_part + key_add)
            return (carry, (query_grad.astype(jnp.bfloat16), key_grad.astype(jnp.bfloat16), grad_values[P_SIZE:].astype(jnp.bfloat16)))
        start = (jnp.zeros((P_SIZE, KVH, DH), jnp.float32), jnp.zeros((P_SIZE, KVH * DH), jnp.float32), jnp.zeros((DH,), jnp.float32), jnp.zeros((DH,), jnp.float32))
        (key_sum, value_sum, query_part, key_part), (query_grads, key_grads, value_grads) = lax.scan(per_response, start, (query_group, key_group, value_group, out_group, length_group))
        prompt_grad, key_extra = norm_back(key_sum, p_unit, p_inverse, key_gain)
        slot = (jnp.arange(RESPS, dtype=jnp.int32) == chosen)[:, None, None]
        blank = jnp.zeros((), jnp.bfloat16)
        out_keys = jnp.where(slot, prompt_grad.astype(jnp.bfloat16)[None], blank)
        out_values = jnp.where(slot, value_sum.astype(jnp.bfloat16)[None], blank)
        return (query_grads, key_grads, value_grads, out_keys, out_values, jnp.stack([query_part, key_part + key_extra]))
    results = lax.map(per_group, (query_raw, key_raw, response_values, prompt_keys, prompt_values, grad_output, lengths, owner))
    gains = lax.optimization_barrier(jnp.sum(results[5], axis=0)) / (GROUPS * RESPS)
    return (results[0], results[1], results[2], results[3], results[4], gains)
```

```python
import functools
import math

import jax
import jax.numpy as jnp
from jax import lax
from jax.experimental import pallas as pl
from jax.experimental.pallas import tpu as pltpu
from jax.sharding import PartitionSpec as P

DH = 128
KVH = 4
QH = 32
L = 256
PROMPT = 1792
T = PROMPT + L
RESPS = 16
GROUPS = 8
EPS = 1e-6
HP = 2
R = HP * L
STEPS = QH // HP
PER = STEPS // KVH
FACT = DH ** -0.5
C2 = FACT * math.log2(math.e)
SUB = 32
AC = 1024
CH = 1024
SAFE = 60.0
f32 = jnp.float32
bf16 = jnp.bfloat16
MESH = pl.DeviceIdType.MESH


def dot(a, b):
    return jnp.dot(a, b, preferred_element_type=f32)


def fold8(x):
    return x.reshape(x.shape[0] // 8, 8, x.shape[1]).sum(0)


def unit_of(x):
    inv = lax.rsqrt(jnp.mean(x * x, axis=-1, keepdims=True) + EPS)
    return x * inv, inv


def norm_grad(grad, raw, gain):
    unit, inv = unit_of(raw)
    du = grad * gain
    return (du - unit * jnp.mean(du * unit, axis=-1, keepdims=True)) * inv, fold8(grad * unit)


HALF = PROMPT // 2
SHARD = PROMPT // 16


def place():
    me = lax.axis_index("resp")
    return me // 4, (me // 2) % 2, me % 2


class Stream:
    def __init__(self, z_first, acc, dst, r0, rz1, rz2, rx, send, recv):
        z, x, c = place()
        self.z_first, self.acc, self.dst = z_first, acc, dst
        self.r0, self.rz1, self.rz2, self.rx, self.send, self.recv = r0, rz1, rz2, rx, send, recv
        self.z, self.x, self.c = z, x, c
        me = z * 4 + x * 2 + c
        self.sib = z * 4 + x * 2 + (1 - c)
        self.xp = z * 4 + (1 - x) * 2 + c
        self.up = ((z + 1) % 4) * 4 + x * 2 + c
        self.down = ((z + 3) % 4) * 4 + x * 2 + c
        if z_first:
            self.zn, self.za, self.xn = 2 * SHARD, SHARD, SHARD
            self.zbase, self.xbase = c * HALF, c * HALF + z * 2 * SHARD
            self.shard = c * HALF + z * 2 * SHARD + x * SHARD
        else:
            self.zn, self.za, self.xn = SHARD, 64, 4 * SHARD
            self.zbase, self.xbase = c * HALF + x * 4 * SHARD, c * HALF
            self.shard = c * HALF + x * 4 * SHARD + z * SHARD

    def copy(self, h, slot, src, dst, who):
        return pltpu.make_async_remote_copy(
            src_ref=src, dst_ref=dst, send_sem=self.send.at[h, slot], recv_sem=self.recv.at[h, slot],
            device_id={"resp": who}, device_id_type=MESH)

    def rows(self, start, n):
        return pl.ds(pl.multiple_of(start, 16), n)

    def piece(self, k):
        return self.zbase + ((self.z + k + 4) % 4) * self.zn

    def add(self, h, start, n, *parts):
        rows = self.rows(start, n)
        total = self.acc[h, rows, :].astype(f32)
        for part in parts:
            total = total + part.astype(f32)
        self.acc[h, rows, :] = total.astype(bf16)

    def copies(self, h, name):
        zn, za, xn, a, d = self.zn, self.za, self.xn, self.acc, self.dst
        if name == "core":
            return [self.copy(h, 0, a.at[h, self.rows((1 - self.c) * HALF, HALF), :], self.r0.at[h], self.sib)]
        if name == "z1":
            o = self.piece(2)
            return [
                self.copy(h, 1, a.at[h, self.rows(o, za), :], self.rz1.at[h, pl.ds(0, za), :], self.up),
                self.copy(h, 2, a.at[h, self.rows(o + za, zn - za), :], self.rz1.at[h, pl.ds(za, zn - za), :], self.down)]
        if name == "z2":
            return [
                self.copy(h, 3, a.at[h, self.rows(self.piece(1), zn), :], self.rz2.at[h, 0], self.up),
                self.copy(h, 4, a.at[h, self.rows(self.piece(3), zn), :], self.rz2.at[h, 1], self.down)]
        if name == "x":
            return [self.copy(h, 5, a.at[h, self.rows(self.xbase + (1 - self.x) * xn, xn), :], self.rx.at[h], self.xp)]
        if name == "gx":
            r = self.rows(self.xbase + self.x * xn, xn)
            return [self.copy(h, 6, d.at[h, r, :], d.at[h, r, :], self.xp)]
        if name == "gz":
            r = self.rows(self.piece(0), zn)
            return [self.copy(h, 7, d.at[h, r, :], d.at[h, r, :], self.up),
                    self.copy(h, 8, d.at[h, r, :], d.at[h, r, :], self.down)]
        if name == "gf":
            r, q = self.rows(self.piece(3), za), self.rows(self.piece(1) + za, zn - za)
            return [self.copy(h, 9, d.at[h, r, :], d.at[h, r, :], self.up),
                    self.copy(h, 10, d.at[h, q, :], d.at[h, q, :], self.down)]
        r = self.rows(self.c * HALF, HALF)
        return [self.copy(h, 11, d.at[h, r, :], d.at[h, r, :], self.sib)]

    def start(self, h, name):
        for one in self.copies(h, name):
            one.start()

    def wait(self, h, name):
        for one in self.copies(h, name):
            one.wait()

    def combine(self, h, name):
        zn, za = self.zn, self.za
        if name == "core":
            self.add(h, self.c * HALF, HALF, self.r0[h])
        elif name == "z1":
            self.add(h, self.piece(1), za, self.rz1[h, :za, :])
            self.add(h, self.piece(3) + za, zn - za, self.rz1[h, za:, :])
        elif name == "z2":
            self.add(h, self.piece(0), zn, self.rz2[h, 0], self.rz2[h, 1])
        elif name == "x":
            self.add(h, self.xbase + self.x * self.xn, self.xn, self.rx[h])

    def order(self):
        if self.z_first:
            return ["core", "z1", "z2", "x", "gx", "gz", "gf", "gcore"]
        return ["core", "x", "z1", "z2", "gz", "gf", "gx", "gcore"]

    def phase(self, h, k, finish):
        names = self.order()
        if k > 0:
            self.wait(h, names[k - 1])
            if k <= 4:
                self.combine(h, names[k - 1])
            if k == 4:
                finish(h, self)
        if k < 8:
            self.start(h, names[k])


PHASES = 9


def stream_scratch(z_first):
    zn, xn = (2 * SHARD, SHARD) if z_first else (SHARD, 4 * SHARD)
    return [
        pltpu.VMEM((KVH, HALF, DH), bf16),
        pltpu.VMEM((KVH, zn, DH), bf16),
        pltpu.VMEM((KVH, 2, zn, DH), bf16),
        pltpu.VMEM((KVH, xn, DH), bf16),
        pltpu.SemaphoreType.DMA((KVH, 12)),
        pltpu.SemaphoreType.DMA((KVH, 12)),
    ]


def greet(barrier, peers_resp, peers_group):
    for p in peers_resp:
        pl.semaphore_signal(barrier, inc=1, device_id={"resp": p}, device_id_type=MESH)
    for p in peers_group:
        pl.semaphore_signal(barrier, inc=1, device_id={"group": p}, device_id_type=MESH)
    pl.semaphore_wait(barrier, len(peers_resp) + len(peers_group))


def others(axis, n):
    me = lax.axis_index(axis)
    return [(me + d) % n for d in range(1, n)]


def exchange(axis, n, buf, send, recv):
    me = lax.axis_index(axis)
    copies = [
        pltpu.make_async_remote_copy(
            src_ref=buf.at[me], dst_ref=buf.at[me], send_sem=send.at[d - 1], recv_sem=recv.at[d - 1],
            device_id={axis: (me + d) % n}, device_id_type=MESH)
        for d in range(1, n)]
    for one in copies:
        one.start()
    return copies


def gather_kernel(kp, vp, kr, vr, kg, mine, ln, kn, vv, raw, live, acc_k, acc_v, lbuf, lsend, lrecv, *scratch):
    keys = Stream(True, acc_k, kn, *scratch[:6])
    values = Stream(False, acc_v, vv, *scratch[6:])
    greet(pltpu.get_barrier_semaphore(), others("resp", RESPS), [])
    me = lax.axis_index("resp")
    lbuf[me] = jnp.zeros((8, DH), f32) + ln[0, 0].astype(f32)
    small = exchange("resp", RESPS, lbuf, lsend, lrecv)
    gain = kg[...]

    def finish_keys(h, s):
        rows = s.rows(s.shard, SHARD)
        x = acc_k[h, rows, :]
        raw[h] = x
        unit, _ = unit_of(x.astype(f32))
        kn[h, rows, :] = (unit * gain).astype(bf16)

    def finish_values(h, s):
        rows = s.rows(s.shard, SHARD)
        vv[h, rows, :] = acc_v[h, rows, :]

    flag = mine[0, 0] > 0
    for h in range(KVH):
        cols = slice(h * DH, (h + 1) * DH)
        acc_k[h] = jnp.where(flag, kp[:, cols], jnp.zeros((), bf16))
        acc_v[h] = jnp.where(flag, vp[:, cols], jnp.zeros((), bf16))
        keys.phase(h, 0, None)
        values.phase(h, 0, None)
    for h in range(KVH):
        cols = slice(h * DH, (h + 1) * DH)
        unit, _ = unit_of(kr[:, cols].astype(f32))
        kn[h, PROMPT:, :] = (unit * gain).astype(bf16)
        vv[h, PROMPT:, :] = vr[:, cols]
    for t in range(1, PHASES + KVH - 1):
        for h in range(KVH):
            if 1 <= t - h < PHASES:
                keys.phase(h, t - h, finish_keys)
                values.phase(h, t - h, finish_values)
    for one in small:
        one.wait()
    live[...] = lbuf[...].sum(0)


def gather(kp, vp, kr, vr, kg, mine, ln):
    vm, sm = pl.BlockSpec(memory_space=pltpu.VMEM), pl.BlockSpec(memory_space=pltpu.SMEM)
    return pl.pallas_call(
        gather_kernel,
        out_shape=(
            jax.ShapeDtypeStruct((KVH, T, DH), bf16),
            jax.ShapeDtypeStruct((KVH, T, DH), bf16),
            jax.ShapeDtypeStruct((KVH, SHARD, DH), bf16),
            jax.ShapeDtypeStruct((8, DH), f32),
        ),
        in_specs=[vm] * 5 + [sm] * 2,
        out_specs=(vm,) * 4,
        scratch_shapes=[
            pltpu.VMEM((KVH, PROMPT, DH), bf16),
            pltpu.VMEM((KVH, PROMPT, DH), bf16),
            pltpu.VMEM((RESPS, 8, DH), f32),
            pltpu.SemaphoreType.DMA((RESPS - 1,)),
            pltpu.SemaphoreType.DMA((RESPS - 1,)),
            *stream_scratch(True),
            *stream_scratch(False),
        ],
        compiler_params=pltpu.CompilerParams(
            collective_id=0, has_side_effects=True, vmem_limit_bytes=56 * 2**20),
    )(kp, vp, kr, vr, kg, mine, ln)


def prepare(h, q_ref, g_ref, gain, live, qt, gt):
    cols = pl.ds(pl.multiple_of(h * DH, DH), DH)
    rows = pl.ds(pl.multiple_of((h % HP) * L, L), L)
    unit, _ = unit_of(q_ref[:, cols].astype(f32))
    qt[h // HP, :, rows] = (unit * gain).T.astype(bf16)
    gt[h // HP, :, rows] = (g_ref[:, cols].astype(f32) * live).T.astype(bf16)


def front_chunk(c, kh, q, g, kn, vv, eb, dp, bias, l, rd):
    x = dot(kn[kh, c * AC:(c + 1) * AC, :], q)
    y = dot(vv[kh, c * AC:(c + 1) * AC, :], g)
    for b in range(AC // SUB):
        lo = c * AC + b * SUB
        rows = slice(lo, lo + SUB)
        xs = x[b * SUB:(b + 1) * SUB] * C2
        if lo >= PROMPT:
            xs = xs + bias[lo - PROMPT:lo - PROMPT + SUB, :]
        ys = y[b * SUB:(b + 1) * SUB]
        e = jnp.exp2(xs)
        eb[rows, :] = e.astype(bf16)
        dp[rows, :] = ys
        l = l + fold8(e)
        rd = rd + fold8(e * ys)
    return l, rd


def front_end(l, rd):
    inv = 1.0 / jnp.sum(l, axis=0, keepdims=True)
    return inv, jnp.sum(rd, axis=0, keepdims=True) * inv


def back_begin(s, inv, qt, gt):
    return (qt[s].astype(f32) * inv).T.astype(bf16), (gt[s].astype(f32) * inv).T.astype(bf16)


def back_chunk(c, kh, rd, q, g, knt, eb, dp, ds, dk, dv, acc):
    rows = slice(c * CH, (c + 1) * CH)
    dv[kh, rows, :] += dot(eb[rows, :], g)
    for b in range(CH // SUB):
        r = slice(c * CH + b * SUB, c * CH + (b + 1) * SUB)
        ds[r, :] = (eb[r, :].astype(f32) * (dp[r, :] - rd)).astype(bf16)
    low = ds[rows, :]
    dk[kh, rows, :] += dot(low, q)
    t = dot(knt[kh, :, rows], low)
    return t if acc is None else acc + t


def finish_query(s, dqt, q_ref, gain, out, gpart):
    for half in range(HP):
        cols = pl.ds(pl.multiple_of((s * HP + half) * DH, DH), DH)
        grad, term = norm_grad(dqt[:, half * L:(half + 1) * L].T, q_ref[:, cols].astype(f32), gain)
        out[:, cols] = grad.astype(bf16)
        gpart[...] += term


def attend_kernel(q_ref, g_ref, kn, vv, kr, qg, kg, live_ref, ln, qo, ko, vo, dk_out, dv_out, part,
                  qt, gt, knt, eb0, eb1, dp0, dp1, ds, bias, dk, dv, gpart):
    q_gain, k_gain = qg[...], kg[...]
    scale = RESPS * L / live_ref[0:1, 0:1]
    live = jnp.where(lax.broadcasted_iota(jnp.int32, (L, 1), 0) < ln[0, 0], scale, 0.0)
    key_row = lax.broadcasted_iota(jnp.int32, (L, R), 0)
    query_row = lax.broadcasted_iota(jnp.int32, (L, R), 1) % L
    bias[...] = jnp.where(key_row <= query_row, 0.0, -1e30)
    gpart[...] = jnp.zeros_like(gpart)
    dk[...] = jnp.zeros_like(dk)
    dv[...] = jnp.zeros_like(dv)

    def prep(h, _):
        prepare(h, q_ref, g_ref, q_gain, live, qt, gt)
        return 0
    lax.fori_loop(0, QH, prep, 0)

    def turn(i, _):
        rows = pl.ds(pl.multiple_of(i * 256, 256), 256)
        for h in range(KVH):
            knt[h, :, rows] = kn[h, rows, :].astype(f32).T.astype(bf16)
        return 0
    lax.fori_loop(0, T // 256, turn, 0)

    ebs, dps = (eb0, eb1), (dp0, dp1)
    l = rd = jnp.zeros((8, R), f32)
    for c in range(T // AC):
        l, rd = front_chunk(c, 0, qt[0], gt[0], kn, vv, eb0, dp0, bias, l, rd)

    def both(i, carry):
        inv, rd = carry
        for par in range(2):
            s = 2 * i + par + 1
            sn = jnp.minimum(s, STEPS - 1)
            prev, now = par, 1 - par
            q2, g2 = back_begin(s - 1, inv, qt, gt)
            q, g = qt[sn], gt[sn]
            l = r = jnp.zeros((8, R), f32)
            acc = None
            for c in range(T // AC):
                l, r = front_chunk(c, sn // PER, q, g, kn, vv, ebs[now], dps[now], bias, l, r)
                acc = back_chunk(c, (s - 1) // PER, rd, q2, g2, knt, ebs[prev], dps[prev], ds, dk, dv, acc)
            finish_query(s - 1, acc * (inv * FACT), q_ref, q_gain, qo, gpart)
            inv, rd = front_end(l, r)
        return inv, rd
    lax.fori_loop(0, STEPS // 2, both, front_end(l, rd))

    terms = jnp.zeros((8, DH), f32)
    for h in range(KVH):
        cols = slice(h * DH, (h + 1) * DH)
        grad, term = norm_grad(dk[h, PROMPT:, :] * FACT, kr[:, cols].astype(f32), k_gain)
        ko[:, cols] = grad.astype(bf16)
        vo[:, cols] = dv[h, PROMPT:, :].astype(bf16)
        terms = terms + term
    row = lax.broadcasted_iota(jnp.int32, (8, DH), 0)
    query_term = jnp.sum(gpart[...], axis=0, keepdims=True)
    key_term = jnp.sum(terms, axis=0, keepdims=True)
    part[...] = jnp.where(row == 0, query_term, 0.0) + jnp.where(row == 1, key_term, 0.0)
    dk_out[...] = (dk[:, :PROMPT, :] * FACT).astype(bf16)
    dv_out[...] = dv[:, :PROMPT, :].astype(bf16)


def attend(q, g, kn, vv, kr, qg, kg, live, ln):
    vm, sm = pl.BlockSpec(memory_space=pltpu.VMEM), pl.BlockSpec(memory_space=pltpu.SMEM)
    return pl.pallas_call(
        attend_kernel,
        out_shape=(
            jax.ShapeDtypeStruct((L, QH * DH), bf16),
            jax.ShapeDtypeStruct((L, KVH * DH), bf16),
            jax.ShapeDtypeStruct((L, KVH * DH), bf16),
            jax.ShapeDtypeStruct((KVH, PROMPT, DH), bf16),
            jax.ShapeDtypeStruct((KVH, PROMPT, DH), bf16),
            jax.ShapeDtypeStruct((8, DH), f32),
        ),
        in_specs=[vm] * 8 + [sm],
        out_specs=(vm,) * 6,
        scratch_shapes=[
            pltpu.VMEM((STEPS, DH, R), bf16),
            pltpu.VMEM((STEPS, DH, R), bf16),
            pltpu.VMEM((KVH, DH, T), bf16),
            pltpu.VMEM((T, R), bf16),
            pltpu.VMEM((T, R), bf16),
            pltpu.VMEM((T, R), f32),
            pltpu.VMEM((T, R), f32),
            pltpu.VMEM((T, R), bf16),
            pltpu.VMEM((L, R), f32),
            pltpu.VMEM((KVH, T, DH), f32),
            pltpu.VMEM((KVH, T, DH), f32),
            pltpu.VMEM((8, DH), f32),
        ],
        compiler_params=pltpu.CompilerParams(vmem_limit_bytes=60 * 2**20),
    )(q, g, kn, vv, kr, qg, kg, live, ln)


def reduce_kernel(dk, dv, raw, kg, part, pk, pv, gains, acc_k, acc_v, gbuf, hbuf, gs, gr, hs, hr, *scratch):
    keys = Stream(True, acc_k, pk, *scratch[:6])
    values = Stream(False, acc_v, pv, *scratch[6:])
    greet(pltpu.get_barrier_semaphore(), others("resp", RESPS), others("group", GROUPS))
    me, group = lax.axis_index("resp"), lax.axis_index("group")
    gain = kg[...]
    terms = []

    def finish_keys(h, s):
        rows = s.rows(s.shard, SHARD)
        g, term = norm_grad(acc_k[h, rows, :].astype(f32), raw[h].astype(f32), gain)
        pk[h, rows, :] = g.astype(bf16)
        terms.append(term)

    def finish_values(h, s):
        rows = s.rows(s.shard, SHARD)
        pv[h, rows, :] = acc_v[h, rows, :]

    for h in range(KVH):
        acc_k[h] = dk[h]
        acc_v[h] = dv[h]
        keys.phase(h, 0, None)
        values.phase(h, 0, None)
    small = []
    for t in range(1, PHASES + KVH - 1):
        for h in range(KVH):
            if 1 <= t - h < PHASES:
                keys.phase(h, t - h, finish_keys)
                values.phase(h, t - h, finish_values)
        if t == 4 + KVH - 1:
            extra = jnp.sum(sum(terms), axis=0, keepdims=True)
            row = lax.broadcasted_iota(jnp.int32, (8, DH), 0)
            gbuf[me] = part[...] + jnp.where(row == 1, extra, 0.0)
            small = exchange("resp", RESPS, gbuf, gs, gr)
        if t == 4 + KVH + 1:
            for one in small:
                one.wait()
            hbuf[group] = gbuf[...].sum(0)
            small = exchange("group", GROUPS, hbuf, hs, hr)
    for one in small:
        one.wait()
    gains[...] = hbuf[...].sum(0) * (1.0 / (RESPS * GROUPS))


def reduce(dk, dv, raw, kg, part):
    vm = pl.BlockSpec(memory_space=pltpu.VMEM)
    return pl.pallas_call(
        reduce_kernel,
        out_shape=(
            jax.ShapeDtypeStruct((KVH, PROMPT, DH), bf16),
            jax.ShapeDtypeStruct((KVH, PROMPT, DH), bf16),
            jax.ShapeDtypeStruct((8, DH), f32),
        ),
        in_specs=[vm] * 5,
        out_specs=(vm,) * 3,
        scratch_shapes=[
            pltpu.VMEM((KVH, PROMPT, DH), bf16),
            pltpu.VMEM((KVH, PROMPT, DH), bf16),
            pltpu.VMEM((RESPS, 8, DH), f32),
            pltpu.VMEM((GROUPS, 8, DH), f32),
            pltpu.SemaphoreType.DMA((RESPS - 1,)),
            pltpu.SemaphoreType.DMA((RESPS - 1,)),
            pltpu.SemaphoreType.DMA((GROUPS - 1,)),
            pltpu.SemaphoreType.DMA((GROUPS - 1,)),
            *stream_scratch(True),
            *stream_scratch(False),
        ],
        compiler_params=pltpu.CompilerParams(
            collective_id=1, has_side_effects=True, vmem_limit_bytes=56 * 2**20),
    )(dk, dv, raw, kg, part)


def spread(value, axis, root):
    mine = lax.axis_index(axis) == root
    return lax.psum(jnp.where(mine, value, jnp.zeros_like(value)), axis)


def normalize(raw, gain):
    values = raw.astype(jnp.float32).reshape(raw.shape[0], -1, DH)
    inverse = lax.rsqrt(jnp.mean(values * values, axis=-1, keepdims=True) + EPS)
    unit = values * inverse
    return (unit, inverse, (unit * gain).astype(jnp.bfloat16))


def norm_back(grad_normed, unit, inverse, gain):
    grad_unit = grad_normed * gain
    grad_raw = (grad_unit - unit * jnp.mean(grad_unit * unit, axis=-1, keepdims=True)) * inverse
    return (grad_raw.reshape(grad_raw.shape[0], -1), jnp.sum(grad_normed * unit, axis=(0, 1)))


def attend_back(queries, key_rows, value_rows, grad_out):
    count = queries.shape[0]
    total = key_rows.shape[0]
    heads = queries.shape[1] // DH
    kv_heads = key_rows.shape[1] // DH
    pairs_per = heads // kv_heads // 2
    allowed = (
        jnp.arange(total, dtype=jnp.int32)[None, :] - (total - count)
        <= jnp.arange(count, dtype=jnp.int32)[:, None]
    )[None]
    factor = DH ** (-0.5)
    query_pairs = jnp.moveaxis(queries.reshape(count, heads // 2, 2, DH), 1, 0)
    out_pairs = jnp.moveaxis(grad_out.reshape(count, heads // 2, 2, DH), 1, 0)
    key_heads = key_rows.reshape(total, kv_heads, DH)
    value_heads = value_rows.reshape(total, kv_heads, DH)

    def one_pair(carry, items):
        grad_keys, grad_values = carry
        pair_index, query_pair, out_pair = items
        shared = pair_index // pairs_per
        key_block = lax.dynamic_index_in_dim(key_heads, shared, 1, keepdims=False)
        value_block = lax.dynamic_index_in_dim(value_heads, shared, 1, keepdims=False)
        scores = (
            jnp.einsum("rhd,kd->hrk", query_pair, key_block, preferred_element_type=jnp.float32)
            * factor
        )
        scores = jnp.where(allowed, scores, -jnp.inf)
        peak = jnp.max(scores, axis=-1, keepdims=True)
        exponent = jnp.exp(scores - peak)
        probs = exponent / jnp.sum(exponent, axis=-1, keepdims=True)
        probs_low = probs.astype(jnp.bfloat16)
        outputs = jnp.einsum(
            "hrk,kd->rhd", probs_low, value_block, preferred_element_type=jnp.float32
        )
        row_dots = jnp.sum(out_pair.astype(jnp.float32) * outputs, axis=-1)
        grad_probs = jnp.einsum(
            "rhd,kd->hrk", out_pair, value_block, preferred_element_type=jnp.float32
        )
        grad_scores = (probs * (grad_probs - jnp.transpose(row_dots)[:, :, None]) * factor).astype(
            jnp.bfloat16
        )
        grad_query = jnp.einsum(
            "hrk,kd->rhd", grad_scores, key_block, preferred_element_type=jnp.float32
        )
        key_add = jnp.einsum(
            "hrk,rhd->kd", grad_scores, query_pair, preferred_element_type=jnp.float32
        )
        value_add = jnp.einsum(
            "hrk,rhd->kd", probs_low, out_pair, preferred_element_type=jnp.float32
        )
        grad_keys = grad_keys.at[shared].add(key_add)
        grad_values = grad_values.at[shared].add(value_add)
        return ((grad_keys, grad_values), grad_query)

    empty = jnp.zeros((kv_heads, total, DH), jnp.float32)
    steps_index = jnp.arange(heads // 2, dtype=jnp.int32)
    (grad_keys, grad_values), grad_queries = lax.scan(
        one_pair, (empty, empty), (steps_index, query_pairs, out_pairs)
    )
    grad_queries = jnp.moveaxis(grad_queries, 0, 1).reshape(count, heads, DH)
    return (grad_queries, jnp.moveaxis(grad_keys, 0, 1), jnp.moveaxis(grad_values, 0, 1))


def plain(
    query_raw,
    key_raw,
    response_values,
    prompt_keys,
    prompt_values,
    grad_output,
    query_gain,
    key_gain,
    lengths,
    owner,
):
    count = query_raw.shape[2]
    prompt_rows = prompt_keys.shape[2]
    width = prompt_keys.shape[3]
    members = lax.axis_size("resp")
    leader = owner[0]
    is_leader = lax.axis_index("resp") == leader
    live_total = lax.psum(lengths.astype(jnp.float32), "resp")
    scaling = members * count / live_total[0, 0]
    prompt_key, prompt_value = (
        spread(prompt_keys[0, 0], "resp", leader),
        spread(prompt_values[0, 0], "resp", leader),
    )
    p_unit, p_inverse, p_normed = normalize(prompt_key, key_gain)
    query_unit, query_inverse, query_normed = normalize(query_raw[0, 0], query_gain)
    key_unit, key_inverse, key_normed = normalize(key_raw[0, 0], key_gain)
    live = (jnp.arange(count, dtype=jnp.int32) < lengths[0, 0])[:, None]
    grad_out = (grad_output[0, 0].astype(jnp.float32) * live * scaling).astype(jnp.bfloat16)
    key_rows = jnp.concatenate([p_normed, key_normed], axis=0).reshape(prompt_rows + count, width)
    value_rows = jnp.concatenate([prompt_value, response_values[0, 0]], axis=0)
    grad_query, grad_keys, grad_values = attend_back(
        query_normed.reshape(count, -1), key_rows, value_rows, grad_out
    )
    query_grad, query_part = norm_back(grad_query, query_unit, query_inverse, query_gain)
    key_grad, key_part = norm_back(grad_keys[prompt_rows:], key_unit, key_inverse, key_gain)
    value_grad = grad_values[prompt_rows:].reshape(count, width)
    key_sum = grad_keys[:prompt_rows].reshape(prompt_rows, width)
    value_sum = grad_values[:prompt_rows].reshape(prompt_rows, width)
    key_total, value_total = lax.psum((key_sum, value_sum), "resp")
    finished, extra = norm_back(key_total.reshape(prompt_rows, -1, DH), p_unit, p_inverse, key_gain)
    key_part = key_part + jnp.where(is_leader, extra, jnp.zeros_like(extra))
    key_low = finished.astype(jnp.bfloat16)
    value_low = value_total.astype(jnp.bfloat16)
    blank = jnp.zeros((), jnp.bfloat16)
    prompt_key_grad = jnp.where(is_leader, key_low, blank)
    prompt_value_grad = jnp.where(is_leader, value_low, blank)
    gains = lax.psum(jnp.stack([query_part, key_part]), ("group", "resp")) / (
        lax.axis_size("group") * members
    )
    return (
        query_grad.astype(jnp.bfloat16)[None, None],
        key_grad.astype(jnp.bfloat16)[None, None],
        value_grad.astype(jnp.bfloat16)[None, None],
        prompt_key_grad[None, None],
        prompt_value_grad[None, None],
        gains,
    )


def fast(query_raw, key_raw, response_values, prompt_keys, prompt_values, grad_output, query_gain, key_gain,
         lengths, owner):
    is_leader = lax.axis_index("resp") == owner[0]
    mine = is_leader.astype(jnp.int32).reshape(1, 1)
    qg, kg = query_gain.reshape(1, DH), key_gain.reshape(1, DH)
    kr = key_raw[0, 0]
    kn, vv, raw, live = gather(prompt_keys[0, 0], prompt_values[0, 0], kr, response_values[0, 0], kg, mine, lengths)
    qo, ko, vo, dk, dv, part = attend(query_raw[0, 0], grad_output[0, 0], kn, vv, kr, qg, kg, live, lengths)
    pk, pv, gains = reduce(dk, dv, raw, kg, part)

    def placed(x):
        rows = jnp.moveaxis(x, 0, 1).reshape(PROMPT, KVH * DH)
        return jnp.where(is_leader, rows, jnp.zeros((), bf16))[None, None]

    return qo[None, None], ko[None, None], vo[None, None], placed(pk), placed(pv), gains[:2]


def body(*args):
    bound = DH ** 0.5 * jnp.max(jnp.abs(args[6] * args[7]))
    return lax.cond(bound <= SAFE, fast, plain, *args)


def solution(mesh):
    in_specs = (
        P("group", "resp", None, None),
        P("group", "resp", None, None),
        P("group", "resp", None, None),
        P("group", "resp", None, None),
        P("group", "resp", None, None),
        P("group", "resp", None, None),
        P(),
        P(),
        P("group", "resp"),
        P("group"),
    )
    out_specs = (
        P("group", "resp", None, None),
        P("group", "resp", None, None),
        P("group", "resp", None, None),
        P("group", "resp", None, None),
        P("group", "resp", None, None),
        P(),
    )
    return jax.shard_map(body, mesh=mesh, in_specs=in_specs, out_specs=out_specs, check_vma=False)
```

```python
import functools
import math

import jax
import jax.numpy as jnp
from jax import lax
from jax.experimental import pallas as pl
from jax.experimental.pallas import tpu as pltpu
from jax.sharding import PartitionSpec as P

DH = 128
KVH = 4
QH = 32
L = 256
PROMPT = 1792
T = PROMPT + L
RESPS = 16
GROUPS = 8
EPS = 1e-6
HP = 2
R = HP * L
STEPS = QH // HP
PER = STEPS // KVH
FACT = DH ** -0.5
C2 = FACT * math.log2(math.e)
SUB = 256
AC = 1024
CH = 1024
SAFE = 60.0
f32 = jnp.float32
bf16 = jnp.bfloat16
MESH = pl.DeviceIdType.MESH


def dot(a, b):
    return jnp.dot(a, b, preferred_element_type=f32)


def fold8(x):
    return x.reshape(x.shape[0] // 8, 8, x.shape[1]).sum(0)


def unit_of(x):
    inv = lax.rsqrt(jnp.mean(x * x, axis=-1, keepdims=True) + EPS)
    return x * inv, inv


def norm_grad(grad, raw, gain):
    unit, inv = unit_of(raw)
    du = grad * gain
    return (du - unit * jnp.mean(du * unit, axis=-1, keepdims=True)) * inv, fold8(grad * unit)


HALF = PROMPT // 2
SHARD = PROMPT // 16


def place():
    me = lax.axis_index("resp")
    return me // 4, (me // 2) % 2, me % 2


CHIPS = [(dz, dx) for dz in range(4) for dx in range(2) if (dz, dx) != (0, 0)]
NEAR = len(CHIPS)


class Stream:
    def __init__(self, acc, dst, flat, r0, rd, send, recv):
        z, x, c = place()
        self.acc, self.dst, self.flat, self.r0, self.rd, self.send, self.recv = acc, dst, flat, r0, rd, send, recv
        self.half = c * HALF
        self.other_half = (1 - c) * HALF
        self.sib = z * 4 + x * 2 + (1 - c)
        self.spots = [((z + dz) % 4) * 2 + (x + dx) % 2 for dz, dx in CHIPS]
        self.peers = [spot * 2 + c for spot in self.spots]
        self.shard = self.half + (z * 2 + x) * SHARD

    def copy(self, h, slot, src, dst, who):
        return pltpu.make_async_remote_copy(
            src_ref=src, dst_ref=dst, send_sem=self.send.at[h, slot], recv_sem=self.recv.at[h, slot],
            device_id={"resp": who}, device_id_type=MESH)

    def rows(self, start, n):
        return pl.ds(pl.multiple_of(start, 16), n)

    def place(self, h, start, n):
        if self.flat:
            return self.dst.at[self.rows(start, n), pl.ds(h * DH, DH)]
        return self.dst.at[h, self.rows(start, n), :]

    def copies(self, h, k):
        a = self.acc
        if k == 0:
            return [self.copy(h, 0, a.at[h, self.rows(self.other_half, HALF), :], self.r0.at[h], self.sib)]
        if k == 1:
            return [
                self.copy(h, 1 + i, a.at[h, self.rows(self.half + self.spots[i] * SHARD, SHARD), :],
                          self.rd.at[h, i], self.peers[i])
                for i in range(NEAR)]
        if k == 2:
            r = self.place(h, self.shard, SHARD)
            return [self.copy(h, 1 + NEAR + i, r, r, self.peers[i]) for i in range(NEAR)]
        r = self.place(h, self.half, HALF)
        return [self.copy(h, 1 + 2 * NEAR, r, r, self.sib)]

    def phase(self, h, k, finish):
        if k > 0:
            for one in self.copies(h, k - 1):
                one.wait()
        if k == 1:
            rows = self.rows(self.half, HALF)
            self.acc[h, rows, :] = (self.acc[h, rows, :].astype(f32) + self.r0[h].astype(f32)).astype(bf16)
        if k == 2:
            total = self.acc[h, self.rows(self.shard, SHARD), :].astype(f32)
            for i in range(NEAR):
                total = total + self.rd[h, i].astype(f32)
            finish(h, self, total)
        if k < 4:
            for one in self.copies(h, k):
                one.start()


PHASES = 5


def stream_scratch():
    return [
        pltpu.VMEM((KVH, HALF, DH), bf16),
        pltpu.VMEM((KVH, NEAR, SHARD, DH), bf16),
        pltpu.SemaphoreType.DMA((KVH, 2 + 2 * NEAR)),
        pltpu.SemaphoreType.DMA((KVH, 2 + 2 * NEAR)),
    ]


def greet(barrier, peers_resp, peers_group):
    for p in peers_resp:
        pl.semaphore_signal(barrier, inc=1, device_id={"resp": p}, device_id_type=MESH)
    for p in peers_group:
        pl.semaphore_signal(barrier, inc=1, device_id={"group": p}, device_id_type=MESH)
    pl.semaphore_wait(barrier, len(peers_resp) + len(peers_group))


def others(axis, n):
    me = lax.axis_index(axis)
    return [(me + d) % n for d in range(1, n)]


def exchange(axis, n, buf, send, recv):
    me = lax.axis_index(axis)
    copies = [
        pltpu.make_async_remote_copy(
            src_ref=buf.at[me], dst_ref=buf.at[me], send_sem=send.at[d - 1], recv_sem=recv.at[d - 1],
            device_id={axis: (me + d) % n}, device_id_type=MESH)
        for d in range(1, n)]
    for one in copies:
        one.start()
    return copies


def gather_kernel(kp, vp, kr, vr, kg, mine, ln, kn, vv, raw, live, acc_k, acc_v, lbuf, lsend, lrecv, *scratch):
    keys = Stream(acc_k, kn, False, *scratch[:4])
    values = Stream(acc_v, vv, False, *scratch[4:])
    greet(pltpu.get_barrier_semaphore(), others("resp", RESPS), [])
    me = lax.axis_index("resp")
    lbuf[me] = jnp.zeros((8, DH), f32) + ln[0, 0].astype(f32)
    small = exchange("resp", RESPS, lbuf, lsend, lrecv)
    gain = kg[...]

    def finish_keys(h, s, x):
        raw[h] = x.astype(bf16)
        unit, _ = unit_of(x)
        kn[h, s.rows(s.shard, SHARD), :] = (unit * gain).astype(bf16)

    def finish_values(h, s, x):
        vv[h, s.rows(s.shard, SHARD), :] = x.astype(bf16)

    flag = mine[0, 0] > 0
    for h in range(KVH):
        cols = slice(h * DH, (h + 1) * DH)
        acc_k[h] = jnp.where(flag, kp[:, cols], jnp.zeros((), bf16))
        acc_v[h] = jnp.where(flag, vp[:, cols], jnp.zeros((), bf16))
        keys.phase(h, 0, None)
        values.phase(h, 0, None)
    for h in range(KVH):
        cols = slice(h * DH, (h + 1) * DH)
        unit, _ = unit_of(kr[:, cols].astype(f32))
        kn[h, PROMPT:, :] = (unit * gain).astype(bf16)
        vv[h, PROMPT:, :] = vr[:, cols]
    for t in range(1, PHASES + KVH - 1):
        for h in range(KVH):
            if 1 <= t - h < PHASES:
                keys.phase(h, t - h, finish_keys)
                values.phase(h, t - h, finish_values)
    for one in small:
        one.wait()
    live[...] = lbuf[...].sum(0)


def gather(kp, vp, kr, vr, kg, mine, ln):
    vm, sm = pl.BlockSpec(memory_space=pltpu.VMEM), pl.BlockSpec(memory_space=pltpu.SMEM)
    return pl.pallas_call(
        gather_kernel,
        out_shape=(
            jax.ShapeDtypeStruct((KVH, T, DH), bf16),
            jax.ShapeDtypeStruct((KVH, T, DH), bf16),
            jax.ShapeDtypeStruct((KVH, SHARD, DH), bf16),
            jax.ShapeDtypeStruct((8, DH), f32),
        ),
        in_specs=[vm] * 5 + [sm] * 2,
        out_specs=(vm,) * 4,
        scratch_shapes=[
            pltpu.VMEM((KVH, PROMPT, DH), bf16),
            pltpu.VMEM((KVH, PROMPT, DH), bf16),
            pltpu.VMEM((RESPS, 8, DH), f32),
            pltpu.SemaphoreType.DMA((RESPS - 1,)),
            pltpu.SemaphoreType.DMA((RESPS - 1,)),
            *stream_scratch(),
            *stream_scratch(),
        ],
        compiler_params=pltpu.CompilerParams(
            collective_id=1, has_side_effects=True, vmem_limit_bytes=56 * 2**20),
    )(kp, vp, kr, vr, kg, mine, ln)


def prepare(h, q_ref, g_ref, gain, live, qt, gt):
    cols = pl.ds(pl.multiple_of(h * DH, DH), DH)
    rows = pl.ds(pl.multiple_of((h % HP) * L, L), L)
    unit, _ = unit_of(q_ref[:, cols].astype(f32))
    qt[h // HP, :, rows] = (unit * gain).T.astype(bf16)
    gt[h // HP, :, rows] = (g_ref[:, cols].astype(f32) * live).T.astype(bf16)


def front_chunk(c, kh, q, g, shift, kn, vv, eb, dp, bias, l, rd):
    x = dot(kn[kh, c * AC:(c + 1) * AC, :], q)
    y = dot(vv[kh, c * AC:(c + 1) * AC, :], g)
    for b in range(AC // SUB):
        lo = c * AC + b * SUB
        rows = slice(lo, lo + SUB)
        xs = x[b * SUB:(b + 1) * SUB] * C2 - shift
        if lo >= PROMPT:
            xs = xs + bias[lo - PROMPT:lo - PROMPT + SUB, :]
        ys = y[b * SUB:(b + 1) * SUB]
        e = jnp.exp2(xs)
        eb[rows, :] = e.astype(bf16)
        dp[rows, :] = ys
        l = l + fold8(e)
        rd = rd + fold8(e * ys)
    return l, rd


def front_end(l, rd):
    inv = 1.0 / jnp.sum(l, axis=0, keepdims=True)
    return inv, jnp.sum(rd, axis=0, keepdims=True) * inv


def back_begin(s, inv, qt, gt):
    return (qt[s].astype(f32) * inv).T.astype(bf16), (gt[s].astype(f32) * inv).T.astype(bf16)


def back_chunk(c, first, kh, slot, rd, q, g, knt, eb, dp, ds, dk, dv, acc):
    rows = slice(c * CH, (c + 1) * CH)
    add_v = dot(eb[rows, :], g)
    for b in range(CH // SUB):
        r = slice(c * CH + b * SUB, c * CH + (b + 1) * SUB)
        ds[r, :] = (eb[r, :].astype(f32) * (dp[r, :] - rd)).astype(bf16)
    low = ds[rows, :]
    add_k = dot(low, q)
    if first:
        dv[slot, rows, :] = add_v
        dk[slot, rows, :] = add_k
    else:
        dv[slot, rows, :] += add_v
        dk[slot, rows, :] += add_k
    t = dot(knt[kh, :, rows], low)
    return t if acc is None else acc + t


def finish_query(s, dqt, q_ref, gain, out, gpart):
    for half in range(HP):
        cols = pl.ds(pl.multiple_of((s * HP + half) * DH, DH), DH)
        grad, term = norm_grad(dqt[:, half * L:(half + 1) * L].T, q_ref[:, cols].astype(f32), gain)
        out[:, cols] = grad.astype(bf16)
        gpart[...] += term


TABLE = [
    [(0, [("in", 1, 2)]), (1, [("out", 0, 0), ("in", 3, 1)]), (2, [("out", 1, 0), ("in", 3, 3)]),
     (3, [("out", 2, 0), ("out", 0, 4)])],
    [(0, [("in", 2, 1)]), (1, [("in", 2, 3), ("out", 0, 1)]), (2, [("out", 1, 1)]),
     (3, [("out", 2, 1), ("out", 1, 3)])],
    [(0, [("in", 1, 3)]), (1, [("in", 3, 2)]), (2, [("in", 3, 4), ("out", 0, 3)]), (3, [("out", 1, 4)])],
    [(0, [("in", 1, 4), ("in", 2, 2)]), (1, [("in", 2, 4), ("out", 0, 2)]), (2, [("out", 1, 2)]),
     (3, [("out", 2, 2)])],
]


def main_kernel(q_hbm, g_hbm, kp, vp, kr, vr, qg, kg, shift, mine, ln,
                qo, ko, vo, pk, pv, gains,
                q_ref, g_ref, acc_k, acc_v, kn, vv, raw, knt, qt, gt, eb0, eb1, dp0, dp1, ds, bias, dk, dv,
                gpart, kpart, lbuf, gbuf, hbuf, load, lsend, lrecv, gs, gr, hs, hr, *scratch):
    in_k = Stream(acc_k, kn, False, *scratch[0:4])
    in_v = Stream(acc_v, vv, False, *scratch[4:8])
    out_k = Stream(acc_k, pk, True, *scratch[8:12])
    out_v = Stream(acc_v, pv, True, *scratch[12:16])
    me, group = lax.axis_index("resp"), lax.axis_index("group")
    q_gain, k_gain = qg[...], kg[...]

    loads = []
    for h in range(KVH):
        cols = pl.ds(h * DH, DH)
        loads.append(pltpu.make_async_copy(kp.at[:, cols], acc_k.at[h], load.at[2 * h]))
        loads.append(pltpu.make_async_copy(vp.at[:, cols], acc_v.at[h], load.at[2 * h + 1]))
    loads.append(pltpu.make_async_copy(g_hbm, g_ref, load.at[2 * KVH]))
    loads.append(pltpu.make_async_copy(q_hbm, q_ref, load.at[2 * KVH + 1]))
    for one in loads:
        one.start()
    lbuf[me] = jnp.zeros((8, DH), f32) + ln[0, 0].astype(f32)
    greet(pltpu.get_barrier_semaphore(), others("resp", RESPS), others("group", GROUPS))
    small = exchange("resp", RESPS, lbuf, lsend, lrecv)

    def shard_in_keys(h, s, x):
        raw[h] = x.astype(bf16)
        unit, _ = unit_of(x)
        kn[h, s.rows(s.shard, SHARD), :] = (unit * k_gain).astype(bf16)

    def shard_in_values(h, s, x):
        vv[h, s.rows(s.shard, SHARD), :] = x.astype(bf16)

    def shard_out_keys(h, s, x):
        grad, term = norm_grad(x, raw[h].astype(f32), k_gain)
        pk[s.rows(s.shard, SHARD), h * DH:(h + 1) * DH] = grad.astype(bf16)
        kpart[...] += term

    def shard_out_values(h, s, x):
        pv[s.rows(s.shard, SHARD), h * DH:(h + 1) * DH] = x.astype(bf16)

    def bring(h, k):
        in_k.phase(h, k, shard_in_keys)
        in_v.phase(h, k, shard_in_values)

    def send_back(h, k):
        out_k.phase(h, k, shard_out_keys)
        out_v.phase(h, k, shard_out_values)

    def turn(h):
        for b in range(0, T, 256):
            knt[h, :, b:b + 256] = kn[h, b:b + 256, :].astype(f32).T.astype(bf16)

    def close_head(h, slot):
        cols = pl.ds(pl.multiple_of(h * DH, DH), DH)
        grad, term = norm_grad(dk[slot, PROMPT:, :] * FACT, kr[:, cols].astype(f32), k_gain)
        ko[:, cols] = grad.astype(bf16)
        vo[:, cols] = dv[slot, PROMPT:, :].astype(bf16)
        kpart[...] += term
        acc_k[h] = (dk[slot, :PROMPT, :] * FACT).astype(bf16)
        acc_v[h] = dv[slot, :PROMPT, :].astype(bf16)

    flag = mine[0, 0] > 0
    for h in range(KVH):
        loads[2 * h].wait()
        loads[2 * h + 1].wait()
        acc_k[h] = jnp.where(flag, acc_k[h], jnp.zeros((), bf16))
        acc_v[h] = jnp.where(flag, acc_v[h], jnp.zeros((), bf16))
        bring(h, 0)
    for h in range(KVH):
        cols = slice(h * DH, (h + 1) * DH)
        unit, _ = unit_of(kr[:, cols].astype(f32))
        kn[h, PROMPT:, :] = (unit * k_gain).astype(bf16)
        vv[h, PROMPT:, :] = vr[:, cols]
    key_row = lax.broadcasted_iota(jnp.int32, (L, R), 0)
    query_row = lax.broadcasted_iota(jnp.int32, (L, R), 1) % L
    bias[...] = jnp.where(key_row <= query_row, 0.0, -1e30)
    gpart[...] = jnp.zeros_like(gpart)
    kpart[...] = jnp.zeros_like(kpart)
    bring(0, 1)
    for one in small:
        one.wait()
    scale = RESPS * L / lbuf[...].sum(0)[0:1, 0:1]
    live = jnp.where(lax.broadcasted_iota(jnp.int32, (L, 1), 0) < ln[0, 0], scale, 0.0)
    loads[2 * KVH].wait()
    loads[2 * KVH + 1].wait()

    def prep(h, _):
        prepare(h, q_ref, g_ref, q_gain, live, qt, gt)
        return 0
    lax.fori_loop(0, QH // 2, prep, 0)
    bring(0, 2)
    lax.fori_loop(QH // 2, QH, prep, 0)
    bring(0, 3)
    bring(1, 1)
    bring(0, 4)

    ebs, dps = (eb0, eb1), (dp0, dp1)
    l = rd = jnp.zeros((8, R), f32)
    for c in range(T // AC):
        l, rd = front_chunk(c, 0, qt[0], gt[0], shift[0], kn, vv, eb0, dp0, bias, l, rd)

    def one_head(kh, carry):
        inv, rd = carry
        slot = kh % 2
        turn(kh)
        for j in range(PER):
            for head, work in TABLE[j]:
                @pl.when(kh == head)
                def _():
                    for act, h, k in work:
                        if act == "in":
                            bring(h, k)
                        else:
                            if k == 0:
                                close_head(h, h % 2)
                            send_back(h, k)

            s = PER * kh + j + 1
            sn = jnp.minimum(s, STEPS - 1)
            prev, now = j % 2, 1 - j % 2
            q2, g2 = back_begin(s - 1, inv, qt, gt)
            q, g, m = qt[sn], gt[sn], shift[sn]
            l = r = jnp.zeros((8, R), f32)
            acc = None
            for c in range(T // AC):
                l, r = front_chunk(c, sn // PER, q, g, m, kn, vv, ebs[now], dps[now], bias, l, r)
                acc = back_chunk(c, j == 0, kh, slot, rd, q2, g2, knt, ebs[prev], dps[prev], ds, dk, dv, acc)
            finish_query(s - 1, acc * (inv * FACT), q_ref, q_gain, qo, gpart)
            inv, rd = front_end(l, r)
        return inv, rd
    lax.fori_loop(0, KVH, one_head, front_end(l, rd))

    close_head(KVH - 1, (KVH - 1) % 2)
    send_back(KVH - 1, 0)
    send_back(KVH - 1, 1)
    send_back(KVH - 2, 3)
    send_back(KVH - 1, 2)
    row = lax.broadcasted_iota(jnp.int32, (8, DH), 0)
    query_term = jnp.sum(gpart[...], axis=0, keepdims=True)
    key_term = jnp.sum(kpart[...], axis=0, keepdims=True)
    gbuf[me] = jnp.where(row == 0, query_term, 0.0) + jnp.where(row == 1, key_term, 0.0)
    small = exchange("resp", RESPS, gbuf, gs, gr)
    send_back(KVH - 2, 4)
    for one in small:
        one.wait()
    hbuf[group] = gbuf[...].sum(0)
    small = exchange("group", GROUPS, hbuf, hs, hr)
    send_back(KVH - 1, 3)
    send_back(KVH - 1, 4)
    for one in small:
        one.wait()
    gains[...] = hbuf[...].sum(0)[:2] * (1.0 / (RESPS * GROUPS))


def attend(q, g, kp, vp, kr, vr, qg, kg, shift, mine, ln):
    vm, sm = pl.BlockSpec(memory_space=pltpu.VMEM), pl.BlockSpec(memory_space=pltpu.SMEM)
    hbm = pl.BlockSpec(memory_space=pl.ANY)
    whole = jax.ShapeDtypeStruct((PROMPT, KVH * DH), bf16)
    pair = lambda n: [pltpu.SemaphoreType.DMA((n,)), pltpu.SemaphoreType.DMA((n,))]
    return pl.pallas_call(
        main_kernel,
        out_shape=(
            jax.ShapeDtypeStruct((L, QH * DH), bf16),
            jax.ShapeDtypeStruct((L, KVH * DH), bf16),
            jax.ShapeDtypeStruct((L, KVH * DH), bf16),
            whole, whole,
            jax.ShapeDtypeStruct((2, DH), f32),
        ),
        in_specs=[hbm] * 4 + [vm] * 5 + [sm] * 2,
        out_specs=(vm,) * 6,
        scratch_shapes=[
            pltpu.VMEM((L, QH * DH), bf16),
            pltpu.VMEM((L, QH * DH), bf16),
            pltpu.VMEM((KVH, PROMPT, DH), bf16),
            pltpu.VMEM((KVH, PROMPT, DH), bf16),
            pltpu.VMEM((KVH, T, DH), bf16),
            pltpu.VMEM((KVH, T, DH), bf16),
            pltpu.VMEM((KVH, SHARD, DH), bf16),
            pltpu.VMEM((KVH, DH, T), bf16),
            pltpu.VMEM((STEPS, DH, R), bf16),
            pltpu.VMEM((STEPS, DH, R), bf16),
            pltpu.VMEM((T, R), bf16),
            pltpu.VMEM((T, R), bf16),
            pltpu.VMEM((T, R), f32),
            pltpu.VMEM((T, R), f32),
            pltpu.VMEM((T, R), bf16),
            pltpu.VMEM((L, R), f32),
            pltpu.VMEM((2, T, DH), f32),
            pltpu.VMEM((2, T, DH), f32),
            pltpu.VMEM((8, DH), f32),
            pltpu.VMEM((8, DH), f32),
            pltpu.VMEM((RESPS, 8, DH), f32),
            pltpu.VMEM((RESPS, 8, DH), f32),
            pltpu.VMEM((GROUPS, 8, DH), f32),
            pltpu.SemaphoreType.DMA((2 * KVH + 2,)),
            *pair(RESPS - 1), *pair(RESPS - 1), *pair(GROUPS - 1),
            *stream_scratch(), *stream_scratch(), *stream_scratch(), *stream_scratch(),
        ],
        compiler_params=pltpu.CompilerParams(
            collective_id=0, has_side_effects=True, vmem_limit_bytes=63 * 2**20),
    )(q, g, kp, vp, kr, vr, qg, kg, shift, mine, ln)


def row_shifts(query, key, prompt_keys, prompt_values, values, qg, kg, mine, ln):
    kn, _, _, _ = gather(prompt_keys, prompt_values, key, values, kg, mine, ln)
    unit, _ = unit_of(query.astype(f32).reshape(L, QH, DH))
    qn = jnp.moveaxis((unit * qg).astype(bf16), 1, 0)
    seen = jnp.arange(T)[None, :] - PROMPT <= jnp.arange(L)[:, None]

    def one(h):
        q = lax.dynamic_index_in_dim(qn, h, 0, keepdims=False)
        k = lax.dynamic_index_in_dim(kn, h // (QH // KVH), 0, keepdims=False)
        scores = jnp.einsum("rd,kd->rk", q, k, preferred_element_type=f32)
        return jnp.max(jnp.where(seen, scores, -jnp.inf), axis=-1)
    return lax.map(one, jnp.arange(QH)).reshape(STEPS, 1, R) * C2


def body(query_raw, key_raw, response_values, prompt_keys, prompt_values, grad_output, query_gain, key_gain,
         lengths, owner):
    is_leader = lax.axis_index("resp") == owner[0]
    mine = is_leader.astype(jnp.int32).reshape(1, 1)
    qg, kg = query_gain.reshape(1, DH), key_gain.reshape(1, DH)
    q, g, kr, vr = query_raw[0, 0], grad_output[0, 0], key_raw[0, 0], response_values[0, 0]
    kp, vp = prompt_keys[0, 0], prompt_values[0, 0]
    bound = DH ** 0.5 * jnp.max(jnp.abs(query_gain * key_gain))
    shift = lax.cond(
        bound <= SAFE, lambda *_: jnp.zeros((STEPS, 1, R), f32), row_shifts,
        q, kr, kp, vp, vr, qg, kg, mine, lengths)
    qo, ko, vo, pk, pv, gains = attend(q, g, kp, vp, kr, vr, qg, kg, shift, mine, lengths)

    def placed(x):
        return jnp.where(is_leader, x, jnp.zeros((), bf16))[None, None]

    return qo[None, None], ko[None, None], vo[None, None], placed(pk), placed(pv), gains


def solution(mesh):
    in_specs = (
        P("group", "resp", None, None),
        P("group", "resp", None, None),
        P("group", "resp", None, None),
        P("group", "resp", None, None),
        P("group", "resp", None, None),
        P("group", "resp", None, None),
        P(),
        P(),
        P("group", "resp"),
        P("group"),
    )
    out_specs = (
        P("group", "resp", None, None),
        P("group", "resp", None, None),
        P("group", "resp", None, None),
        P("group", "resp", None, None),
        P("group", "resp", None, None),
        P(),
    )
    return jax.shard_map(body, mesh=mesh, in_specs=in_specs, out_specs=out_specs, check_vma=False)
```

```python
import functools
import math

import jax
import jax.numpy as jnp
from jax import lax
from jax.experimental import pallas as pl
from jax.experimental.pallas import tpu as pltpu
from jax.sharding import PartitionSpec as P

DH = 128
KVH = 4
QH = 32
L = 256
PROMPT = 1792
T = PROMPT + L
RESPS = 16
GROUPS = 8
EPS = 1e-6
HP = 2
R = HP * L
STEPS = QH // HP
PER = STEPS // KVH
FACT = DH ** -0.5
C2 = FACT * math.log2(math.e)
SUB = 256
AC = 1024
CH = 1024
SAFE = 60.0
f32 = jnp.float32
bf16 = jnp.bfloat16
MESH = pl.DeviceIdType.MESH


def dot(a, b):
    return jnp.dot(a, b, preferred_element_type=f32)


def fold8(x):
    return x.reshape(x.shape[0] // 8, 8, x.shape[1]).sum(0)


def unit_of(x):
    inv = lax.rsqrt(jnp.mean(x * x, axis=-1, keepdims=True) + EPS)
    return x * inv, inv


def norm_grad(grad, raw, gain):
    unit, inv = unit_of(raw)
    du = grad * gain
    return (du - unit * jnp.mean(du * unit, axis=-1, keepdims=True)) * inv, fold8(grad * unit)


HALF = PROMPT // 2
SHARD = PROMPT // 16


def place():
    me = lax.axis_index("resp")
    return me // 4, (me // 2) % 2, me % 2


CHIPS = [(dz, dx) for dz in range(4) for dx in range(2) if (dz, dx) != (0, 0)]
NEAR = len(CHIPS)


class Stream:
    def __init__(self, acc, dst, flat, r0, rd, send, recv):
        z, x, c = place()
        self.acc, self.dst, self.flat, self.r0, self.rd, self.send, self.recv = acc, dst, flat, r0, rd, send, recv
        self.half = c * HALF
        self.other_half = (1 - c) * HALF
        self.sib = z * 4 + x * 2 + (1 - c)
        self.spots = [((z + dz) % 4) * 2 + (x + dx) % 2 for dz, dx in CHIPS]
        self.peers = [spot * 2 + c for spot in self.spots]
        self.shard = self.half + (z * 2 + x) * SHARD

    def copy(self, h, slot, src, dst, who):
        return pltpu.make_async_remote_copy(
            src_ref=src, dst_ref=dst, send_sem=self.send.at[h, slot], recv_sem=self.recv.at[h, slot],
            device_id={"resp": who}, device_id_type=MESH)

    def rows(self, start, n):
        return pl.ds(pl.multiple_of(start, 16), n)

    def place(self, h, start, n):
        if self.flat:
            return self.dst.at[self.rows(start, n), pl.ds(h * DH, DH)]
        return self.dst.at[h, self.rows(start, n), :]

    def copies(self, h, k):
        a = self.acc
        if k == 0:
            return [self.copy(h, 0, a.at[h, self.rows(self.other_half, HALF), :], self.r0.at[h], self.sib)]
        if k == 1:
            return [
                self.copy(h, 1 + i, a.at[h, self.rows(self.half + self.spots[i] * SHARD, SHARD), :],
                          self.rd.at[h, i], self.peers[i])
                for i in range(NEAR)]
        if k == 2:
            r = self.place(h, self.shard, SHARD)
            return [self.copy(h, 1 + NEAR + i, r, r, self.peers[i]) for i in range(NEAR)]
        r = self.place(h, self.half, HALF)
        return [self.copy(h, 1 + 2 * NEAR, r, r, self.sib)]

    def phase(self, h, k, finish):
        if k > 0:
            for one in self.copies(h, k - 1):
                one.wait()
        if k == 1:
            rows = self.rows(self.half, HALF)
            self.acc[h, rows, :] = (self.acc[h, rows, :].astype(f32) + self.r0[h].astype(f32)).astype(bf16)
        if k == 2:
            total = self.acc[h, self.rows(self.shard, SHARD), :].astype(f32)
            for i in range(NEAR):
                total = total + self.rd[h, i].astype(f32)
            finish(h, self, total)
        if k < 4:
            for one in self.copies(h, k):
                one.start()


PHASES = 5


def stream_scratch():
    return [
        pltpu.VMEM((KVH, HALF, DH), bf16),
        pltpu.VMEM((KVH, NEAR, SHARD, DH), bf16),
        pltpu.SemaphoreType.DMA((KVH, 2 + 2 * NEAR)),
        pltpu.SemaphoreType.DMA((KVH, 2 + 2 * NEAR)),
    ]


def greet(barrier, peers_resp, peers_group):
    for p in peers_resp:
        pl.semaphore_signal(barrier, inc=1, device_id={"resp": p}, device_id_type=MESH)
    for p in peers_group:
        pl.semaphore_signal(barrier, inc=1, device_id={"group": p}, device_id_type=MESH)
    pl.semaphore_wait(barrier, len(peers_resp) + len(peers_group))


def others(axis, n):
    me = lax.axis_index(axis)
    return [(me + d) % n for d in range(1, n)]


def exchange(axis, n, buf, send, recv):
    me = lax.axis_index(axis)
    copies = [
        pltpu.make_async_remote_copy(
            src_ref=buf.at[me], dst_ref=buf.at[me], send_sem=send.at[d - 1], recv_sem=recv.at[d - 1],
            device_id={axis: (me + d) % n}, device_id_type=MESH)
        for d in range(1, n)]
    for one in copies:
        one.start()
    return copies


def gather_kernel(kp, vp, kr, vr, kg, mine, ln, kn, vv, raw, live, acc_k, acc_v, lbuf, lsend, lrecv, *scratch):
    keys = Stream(acc_k, kn, False, *scratch[:4])
    values = Stream(acc_v, vv, False, *scratch[4:])
    greet(pltpu.get_barrier_semaphore(), others("resp", RESPS), [])
    me = lax.axis_index("resp")
    lbuf[me] = jnp.zeros((8, DH), f32) + ln[0, 0].astype(f32)
    small = exchange("resp", RESPS, lbuf, lsend, lrecv)
    gain = kg[...]

    def finish_keys(h, s, x):
        raw[h] = x.astype(bf16)
        unit, _ = unit_of(x)
        kn[h, s.rows(s.shard, SHARD), :] = (unit * gain).astype(bf16)

    def finish_values(h, s, x):
        vv[h, s.rows(s.shard, SHARD), :] = x.astype(bf16)

    flag = mine[0, 0] > 0
    for h in range(KVH):
        cols = slice(h * DH, (h + 1) * DH)
        acc_k[h] = jnp.where(flag, kp[:, cols], jnp.zeros((), bf16))
        acc_v[h] = jnp.where(flag, vp[:, cols], jnp.zeros((), bf16))
        keys.phase(h, 0, None)
        values.phase(h, 0, None)
    for h in range(KVH):
        cols = slice(h * DH, (h + 1) * DH)
        unit, _ = unit_of(kr[:, cols].astype(f32))
        kn[h, PROMPT:, :] = (unit * gain).astype(bf16)
        vv[h, PROMPT:, :] = vr[:, cols]
    for t in range(1, PHASES + KVH - 1):
        for h in range(KVH):
            if 1 <= t - h < PHASES:
                keys.phase(h, t - h, finish_keys)
                values.phase(h, t - h, finish_values)
    for one in small:
        one.wait()
    live[...] = lbuf[...].sum(0)


def gather(kp, vp, kr, vr, kg, mine, ln):
    vm, sm = pl.BlockSpec(memory_space=pltpu.VMEM), pl.BlockSpec(memory_space=pltpu.SMEM)
    return pl.pallas_call(
        gather_kernel,
        out_shape=(
            jax.ShapeDtypeStruct((KVH, T, DH), bf16),
            jax.ShapeDtypeStruct((KVH, T, DH), bf16),
            jax.ShapeDtypeStruct((KVH, SHARD, DH), bf16),
            jax.ShapeDtypeStruct((8, DH), f32),
        ),
        in_specs=[vm] * 5 + [sm] * 2,
        out_specs=(vm,) * 4,
        scratch_shapes=[
            pltpu.VMEM((KVH, PROMPT, DH), bf16),
            pltpu.VMEM((KVH, PROMPT, DH), bf16),
            pltpu.VMEM((RESPS, 8, DH), f32),
            pltpu.SemaphoreType.DMA((RESPS - 1,)),
            pltpu.SemaphoreType.DMA((RESPS - 1,)),
            *stream_scratch(),
            *stream_scratch(),
        ],
        compiler_params=pltpu.CompilerParams(
            collective_id=1, has_side_effects=True, vmem_limit_bytes=56 * 2**20),
    )(kp, vp, kr, vr, kg, mine, ln)


def prepare(h, q_ref, g_ref, gain, live, qt, gt):
    cols = pl.ds(pl.multiple_of(h * DH, DH), DH)
    rows = pl.ds(pl.multiple_of((h % HP) * L, L), L)
    unit, _ = unit_of(q_ref[:, cols].astype(f32))
    qt[h // HP, :, rows] = (unit * gain).T.astype(bf16)
    gt[h // HP, :, rows] = (g_ref[:, cols].astype(f32) * live).T.astype(bf16)


def front_chunk(c, kh, q, g, shift, kn, vv, eb, dp, bias, l, rd):
    x = dot(kn[kh, c * AC:(c + 1) * AC, :], q)
    y = dot(vv[kh, c * AC:(c + 1) * AC, :], g)
    for b in range(AC // SUB):
        lo = c * AC + b * SUB
        rows = slice(lo, lo + SUB)
        xs = x[b * SUB:(b + 1) * SUB] * C2 - shift
        if lo >= PROMPT:
            xs = xs + bias[lo - PROMPT:lo - PROMPT + SUB, :]
        ys = y[b * SUB:(b + 1) * SUB]
        e = jnp.exp2(xs)
        eb[rows, :] = e.astype(bf16)
        dp[rows, :] = ys
        l = l + fold8(e)
        rd = rd + fold8(e * ys)
    return l, rd


def front_end(l, rd):
    inv = 1.0 / jnp.sum(l, axis=0, keepdims=True)
    return inv, jnp.sum(rd, axis=0, keepdims=True) * inv


def back_begin(s, inv, qt, gt):
    return (qt[s].astype(f32) * inv).T.astype(bf16), (gt[s].astype(f32) * inv).T.astype(bf16)


def back_chunk(c, first, kh, slot, rd, q, g, knt, eb, dp, ds, dk, dv, acc):
    rows = slice(c * CH, (c + 1) * CH)
    add_v = dot(eb[rows, :], g)
    for b in range(CH // SUB):
        r = slice(c * CH + b * SUB, c * CH + (b + 1) * SUB)
        ds[r, :] = (eb[r, :].astype(f32) * (dp[r, :] - rd)).astype(bf16)
    low = ds[rows, :]
    add_k = dot(low, q)
    if first:
        dv[slot, rows, :] = add_v
        dk[slot, rows, :] = add_k
    else:
        dv[slot, rows, :] += add_v
        dk[slot, rows, :] += add_k
    t = dot(knt[kh, :, rows], low)
    return t if acc is None else acc + t


def finish_query(s, dqt, q_ref, gain, out, gpart):
    for half in range(HP):
        cols = pl.ds(pl.multiple_of((s * HP + half) * DH, DH), DH)
        grad, term = norm_grad(dqt[:, half * L:(half + 1) * L].T, q_ref[:, cols].astype(f32), gain)
        out[:, cols] = grad.astype(bf16)
        gpart[...] += term


TABLE = {
    0: [("in", 1, 2), ("in", 2, 1)],
    2: [("in", 1, 3)],
    3: [("in", 1, 4), ("in", 2, 2), ("in", 3, 1)],
    4: [("out", 0, 0)],
    6: [("in", 2, 3), ("in", 3, 2), ("out", 0, 1)],
    7: [("in", 2, 4)],
    8: [("out", 1, 0)],
    9: [("in", 3, 3), ("out", 0, 2), ("out", 1, 1)],
    10: [("in", 3, 4)],
    12: [("out", 0, 3), ("out", 1, 2), ("out", 2, 0)],
    13: [("out", 0, 4), ("out", 2, 1)],
    15: [("out", 1, 3)],
}


def main_kernel(q_hbm, g_hbm, kp, vp, kr, vr, qg, kg, shift, mine, ln,
                qo_hbm, ko, vo, pk, pv, gains,
                qo, q_ref, g_ref, acc_k, acc_v, kn, vv, raw, knt, qt, gt, eb0, eb1, dp0, dp1, ds, bias, dk, dv,
                gpart, kpart, lbuf, gbuf, hbuf, load, lsend, lrecv, gs, gr, hs, hr, *scratch):
    in_k = Stream(acc_k, kn, False, *scratch[0:4])
    in_v = Stream(acc_v, vv, False, *scratch[4:8])
    out_k = Stream(acc_k, pk, True, *scratch[8:12])
    out_v = Stream(acc_v, pv, True, *scratch[12:16])
    me, group = lax.axis_index("resp"), lax.axis_index("group")
    q_gain, k_gain = qg[...], kg[...]

    loads = []
    for h in range(KVH):
        cols = pl.ds(h * DH, DH)
        loads.append(pltpu.make_async_copy(kp.at[:, cols], acc_k.at[h], load.at[2 * h]))
        loads.append(pltpu.make_async_copy(vp.at[:, cols], acc_v.at[h], load.at[2 * h + 1]))
    loads.append(pltpu.make_async_copy(g_hbm, g_ref, load.at[2 * KVH]))
    loads.append(pltpu.make_async_copy(q_hbm, q_ref, load.at[2 * KVH + 1]))
    for one in loads:
        one.start()
    lbuf[me] = jnp.zeros((8, DH), f32) + ln[0, 0].astype(f32)
    greet(pltpu.get_barrier_semaphore(), others("resp", RESPS), others("group", GROUPS))
    small = exchange("resp", RESPS, lbuf, lsend, lrecv)

    def shard_in_keys(h, s, x):
        raw[h] = x.astype(bf16)
        unit, _ = unit_of(x)
        kn[h, s.rows(s.shard, SHARD), :] = (unit * k_gain).astype(bf16)

    def shard_in_values(h, s, x):
        vv[h, s.rows(s.shard, SHARD), :] = x.astype(bf16)

    shared = []

    def shard_out_keys(h, s, x):
        grad, term = norm_grad(x, raw[h].astype(f32), k_gain)
        pk[s.rows(s.shard, SHARD), h * DH:(h + 1) * DH] = grad.astype(bf16)
        kpart[...] += term
        if isinstance(h, int) and h == KVH - 1:
            shared.extend(share_gains())

    def share_gains():
        row = lax.broadcasted_iota(jnp.int32, (8, DH), 0)
        query_term = jnp.sum(gpart[...], axis=0, keepdims=True)
        key_term = jnp.sum(kpart[...], axis=0, keepdims=True)
        gbuf[me] = jnp.where(row == 0, query_term, 0.0) + jnp.where(row == 1, key_term, 0.0)
        return exchange("resp", RESPS, gbuf, gs, gr)

    def shard_out_values(h, s, x):
        pv[s.rows(s.shard, SHARD), h * DH:(h + 1) * DH] = x.astype(bf16)

    def bring(h, k):
        in_k.phase(h, k, shard_in_keys)
        in_v.phase(h, k, shard_in_values)

    def send_back(h, k):
        out_k.phase(h, k, shard_out_keys)
        out_v.phase(h, k, shard_out_values)

    def turn(h):
        for b in range(0, T, 256):
            knt[h, :, b:b + 256] = kn[h, b:b + 256, :].astype(f32).T.astype(bf16)

    def close_head(h, slot):
        cols = pl.ds(pl.multiple_of(h * DH, DH), DH)
        grad, term = norm_grad(dk[slot, PROMPT:, :] * FACT, kr[:, cols].astype(f32), k_gain)
        ko[:, cols] = grad.astype(bf16)
        vo[:, cols] = dv[slot, PROMPT:, :].astype(bf16)
        kpart[...] += term
        acc_k[h] = (dk[slot, :PROMPT, :] * FACT).astype(bf16)
        acc_v[h] = dv[slot, :PROMPT, :].astype(bf16)

    flag = mine[0, 0] > 0
    for h in range(KVH):
        loads[2 * h].wait()
        loads[2 * h + 1].wait()
        acc_k[h] = jnp.where(flag, acc_k[h], jnp.zeros((), bf16))
        acc_v[h] = jnp.where(flag, acc_v[h], jnp.zeros((), bf16))
        bring(h, 0)
    for h in range(KVH):
        cols = slice(h * DH, (h + 1) * DH)
        unit, _ = unit_of(kr[:, cols].astype(f32))
        kn[h, PROMPT:, :] = (unit * k_gain).astype(bf16)
        vv[h, PROMPT:, :] = vr[:, cols]
    key_row = lax.broadcasted_iota(jnp.int32, (L, R), 0)
    query_row = lax.broadcasted_iota(jnp.int32, (L, R), 1) % L
    bias[...] = jnp.where(key_row <= query_row, 0.0, -1e30)
    gpart[...] = jnp.zeros_like(gpart)
    kpart[...] = jnp.zeros_like(kpart)
    bring(0, 1)
    for one in small:
        one.wait()
    scale = RESPS * L / lbuf[...].sum(0)[0:1, 0:1]
    live = jnp.where(lax.broadcasted_iota(jnp.int32, (L, 1), 0) < ln[0, 0], scale, 0.0)
    loads[2 * KVH].wait()
    loads[2 * KVH + 1].wait()

    def prep(h, _):
        prepare(h, q_ref, g_ref, q_gain, live, qt, gt)
        return 0
    lax.fori_loop(0, QH // 2, prep, 0)
    bring(0, 2)
    lax.fori_loop(QH // 2, QH, prep, 0)
    bring(0, 3)
    bring(1, 1)
    bring(0, 4)

    ebs, dps = (eb0, eb1), (dp0, dp1)
    l = rd = jnp.zeros((8, R), f32)
    for c in range(T // AC):
        l, rd = front_chunk(c, 0, qt[0], gt[0], shift[0], kn, vv, eb0, dp0, bias, l, rd)

    def one_head(kh, carry):
        inv, rd = carry
        slot = kh % 2
        turn(kh)
        for j in range(PER):
            for n, work in TABLE.items():
                if n % PER != j:
                    continue

                @pl.when(kh == n // PER)
                def _():
                    for way, h, k in work:
                        if way == "in":
                            bring(h, k)
                        else:
                            if k == 0:
                                close_head(h, h % 2)
                            send_back(h, k)

            s = PER * kh + j + 1
            sn = jnp.minimum(s, STEPS - 1)
            prev, now = j % 2, 1 - j % 2
            q2, g2 = back_begin(s - 1, inv, qt, gt)
            q, g, m = qt[sn], gt[sn], shift[sn]
            l = r = jnp.zeros((8, R), f32)
            acc = None
            for c in range(T // AC):
                l, r = front_chunk(c, sn // PER, q, g, m, kn, vv, ebs[now], dps[now], bias, l, r)
                acc = back_chunk(c, j == 0, kh, slot, rd, q2, g2, knt, ebs[prev], dps[prev], ds, dk, dv, acc)
            finish_query(s - 1, acc * (inv * FACT), q_ref, q_gain, qo, gpart)
            inv, rd = front_end(l, r)
        return inv, rd
    lax.fori_loop(0, KVH, one_head, front_end(l, rd))

    keep = pltpu.make_async_copy(qo, qo_hbm, load.at[0])
    keep.start()
    close_head(KVH - 1, (KVH - 1) % 2)
    send_back(KVH - 1, 0)
    send_back(KVH - 2, 2)
    send_back(KVH - 1, 1)
    send_back(KVH - 3, 4)
    send_back(KVH - 2, 3)
    send_back(KVH - 1, 2)
    small = shared
    send_back(KVH - 2, 4)
    for one in small:
        one.wait()
    hbuf[group] = gbuf[...].sum(0)
    small = exchange("group", GROUPS, hbuf, hs, hr)
    send_back(KVH - 1, 3)
    send_back(KVH - 1, 4)
    pk[...] = jnp.where(flag, pk[...], jnp.zeros((), bf16))
    pv[...] = jnp.where(flag, pv[...], jnp.zeros((), bf16))
    for one in small:
        one.wait()
    keep.wait()
    gains[...] = hbuf[...].sum(0)[:2] * (1.0 / (RESPS * GROUPS))


def attend(q, g, kp, vp, kr, vr, qg, kg, shift, mine, ln):
    vm, sm = pl.BlockSpec(memory_space=pltpu.VMEM), pl.BlockSpec(memory_space=pltpu.SMEM)
    hbm = pl.BlockSpec(memory_space=pl.ANY)
    whole = jax.ShapeDtypeStruct((PROMPT, KVH * DH), bf16)
    pair = lambda n: [pltpu.SemaphoreType.DMA((n,)), pltpu.SemaphoreType.DMA((n,))]
    return pl.pallas_call(
        main_kernel,
        out_shape=(
            jax.ShapeDtypeStruct((L, QH * DH), bf16),
            jax.ShapeDtypeStruct((L, KVH * DH), bf16),
            jax.ShapeDtypeStruct((L, KVH * DH), bf16),
            whole, whole,
            jax.ShapeDtypeStruct((2, DH), f32),
        ),
        in_specs=[hbm] * 4 + [vm] * 5 + [sm] * 2,
        out_specs=(hbm,) + (vm,) * 5,
        scratch_shapes=[
            pltpu.VMEM((L, QH * DH), bf16),
            pltpu.VMEM((L, QH * DH), bf16),
            pltpu.VMEM((L, QH * DH), bf16),
            pltpu.VMEM((KVH, PROMPT, DH), bf16),
            pltpu.VMEM((KVH, PROMPT, DH), bf16),
            pltpu.VMEM((KVH, T, DH), bf16),
            pltpu.VMEM((KVH, T, DH), bf16),
            pltpu.VMEM((KVH, SHARD, DH), bf16),
            pltpu.VMEM((KVH, DH, T), bf16),
            pltpu.VMEM((STEPS, DH, R), bf16),
            pltpu.VMEM((STEPS, DH, R), bf16),
            pltpu.VMEM((T, R), bf16),
            pltpu.VMEM((T, R), bf16),
            pltpu.VMEM((T, R), f32),
            pltpu.VMEM((T, R), f32),
            pltpu.VMEM((T, R), bf16),
            pltpu.VMEM((L, R), f32),
            pltpu.VMEM((2, T, DH), f32),
            pltpu.VMEM((2, T, DH), f32),
            pltpu.VMEM((8, DH), f32),
            pltpu.VMEM((8, DH), f32),
            pltpu.VMEM((RESPS, 8, DH), f32),
            pltpu.VMEM((RESPS, 8, DH), f32),
            pltpu.VMEM((GROUPS, 8, DH), f32),
            pltpu.SemaphoreType.DMA((2 * KVH + 2,)),
            *pair(RESPS - 1), *pair(RESPS - 1), *pair(GROUPS - 1),
            *stream_scratch(), *stream_scratch(), *stream_scratch(), *stream_scratch(),
        ],
        compiler_params=pltpu.CompilerParams(
            collective_id=0, has_side_effects=True, vmem_limit_bytes=63 * 2**20),
    )(q, g, kp, vp, kr, vr, qg, kg, shift, mine, ln)


def row_shifts(query, key, prompt_keys, prompt_values, values, qg, kg, mine, ln):
    kn, _, _, _ = gather(prompt_keys, prompt_values, key, values, kg, mine, ln)
    unit, _ = unit_of(query.astype(f32).reshape(L, QH, DH))
    qn = jnp.moveaxis((unit * qg).astype(bf16), 1, 0)
    seen = jnp.arange(T)[None, :] - PROMPT <= jnp.arange(L)[:, None]

    def one(h):
        q = lax.dynamic_index_in_dim(qn, h, 0, keepdims=False)
        k = lax.dynamic_index_in_dim(kn, h // (QH // KVH), 0, keepdims=False)
        scores = jnp.einsum("rd,kd->rk", q, k, preferred_element_type=f32)
        return jnp.max(jnp.where(seen, scores, -jnp.inf), axis=-1)
    return lax.map(one, jnp.arange(QH)).reshape(STEPS, 1, R) * C2


def body(query_raw, key_raw, response_values, prompt_keys, prompt_values, grad_output, query_gain, key_gain,
         lengths, owner):
    is_leader = lax.axis_index("resp") == owner[0]
    mine = is_leader.astype(jnp.int32).reshape(1, 1)
    qg, kg = query_gain.reshape(1, DH), key_gain.reshape(1, DH)
    q, g, kr, vr = query_raw[0, 0], grad_output[0, 0], key_raw[0, 0], response_values[0, 0]
    kp, vp = prompt_keys[0, 0], prompt_values[0, 0]
    bound = DH ** 0.5 * jnp.max(jnp.abs(query_gain * key_gain))
    shift = lax.cond(
        bound <= SAFE, lambda *_: jnp.zeros((STEPS, 1, R), f32), row_shifts,
        q, kr, kp, vp, vr, qg, kg, mine, lengths)
    qo, ko, vo, pk, pv, gains = attend(q, g, kp, vp, kr, vr, qg, kg, shift, mine, lengths)

    return qo[None, None], ko[None, None], vo[None, None], pk[None, None], pv[None, None], gains


def solution(mesh):
    in_specs = (
        P("group", "resp", None, None),
        P("group", "resp", None, None),
        P("group", "resp", None, None),
        P("group", "resp", None, None),
        P("group", "resp", None, None),
        P("group", "resp", None, None),
        P(),
        P(),
        P("group", "resp"),
        P("group"),
    )
    out_specs = (
        P("group", "resp", None, None),
        P("group", "resp", None, None),
        P("group", "resp", None, None),
        P("group", "resp", None, None),
        P("group", "resp", None, None),
        P(),
    )
    return jax.shard_map(body, mesh=mesh, in_specs=in_specs, out_specs=out_specs, check_vma=False)
```
